128 devices in a mesh: rep: 4 (over z_hi, core), fsdp: 32 (over z_lo, x, y).
Axes of the slice: x: 4, y: 4, z: 4 (z_hi: 2, z_lo: 2; z = z_hi * 2 + z_lo), core: 2. Of those that a mesh axis runs over, the one named last changes fastest.
Arguments:
- layer_input: bfloat16 [4, 16384, 8192], P('rep', 'fsdp'), may hold values from -512 to 512
- value_weight: bfloat16 [4, 8192, 512], P('rep', 'fsdp'), may hold values from -6 to 6
- norm_gain: bfloat16 [4, 8192], P('rep', 'fsdp'), may hold values from 0.25 to 1.75
- cotangent: bfloat16 [4, 16384, 512], P('rep', 'fsdp'), may hold values from -6 to 6
- frag_global: float32 [8192, 1024], P('fsdp'), may hold values from -6 to 6
- frag_momentum: float32 [8192, 1024], P('fsdp'), may hold values from -3 to 3
- frag_snapshot: bfloat16 [4, 8192, 1024], P('rep', 'fsdp'), may hold values from -6 to 6
- frag_local: bfloat16 [4, 8192, 1024], P('rep', 'fsdp'), may hold values from -6 to 6
Outputs:
- values: bfloat16 [4, 16384, 512], P('rep', 'fsdp')
- input_grad: bfloat16 [4, 16384, 8192], P('rep', 'fsdp')
- weight_grad: float32 [4, 8192, 512], P('rep', 'fsdp')
- new_global: float32 [8192, 1024], P('fsdp')
- new_momentum: float32 [8192, 1024], P('fsdp')
- new_local: bfloat16 [4, 8192, 1024], P('rep', 'fsdp')
The draws below stay inside these ranges and needn't reach their ends.
All inputs are finite; a program needn't handle non-finite values.
Results may differ from the reference program's by a relative error of at most 0.005.
Values may be sent and summed in bfloat16 or wider, within the bound.
No kernel may reach another device: no remote copies, remote signals or barrier semaphores. Data moves between devices by JAX's collectives and lax.ppermute only.
A program may use at most 192 MiB of HBM per device.

```python
import math
import jax
import jax.numpy as jnp
from jax import lax

D = 8192
KV = 512
TOKENS = 16384
REPLICAS = 4
FRAG = 1024


def draw_layer_input(key, part):
    key = jax.random.fold_in(key, 11)
    key_base, key_cols, key_rows = jax.random.split(key, 3)
    shape = (REPLICAS, TOKENS, D)
    column_scale = jnp.exp(jax.random.uniform(key_cols, (1, 1, D), jnp.float32, 0.0, math.log(10.0)))
    row_scale = jnp.exp(jax.random.uniform(key_rows, (REPLICAS, TOKENS, 1), jnp.float32, 0.0, math.log(10.0)))
    base = jnp.clip(jax.random.normal(key_base, shape, jnp.float32), -4.0, 4.0)
    return (base * row_scale * column_scale).astype(jnp.bfloat16)


def block_levels(key, dims, pieces, least, top_value):
    level = 1.0
    for position, blocks in pieces:
        draws = jax.random.uniform(jax.random.fold_in(jax.random.fold_in(key, 6), position), (blocks,), jnp.float32, least / len(pieces), top_value / len(pieces))
        level = level * jnp.repeat(jnp.exp(draws), dims[position] // blocks).reshape((-1,) + (1,) * (len(dims) - 1 - position))
    return level


def scatter_about(stream_key, shape, deviation, bound, shards=(), kind=jnp.bfloat16):
    entries = jax.random.normal(stream_key, shape, jnp.float32) * deviation
    if len(shards) > 0:
        entries = block_levels(stream_key, shape, shards, -0.22, 0.18) * entries
    return jnp.clip(entries, min=-bound, max=bound).astype(kind)


def setup_inputs(seed: int = 0) -> dict:
    arg_keys = jax.random.split(jax.random.key(seed), 9)
    return {
        "layer_input": draw_layer_input(jax.random.fold_in(arg_keys[8], 71), 0),
        "value_weight": scatter_about(arg_keys[1], (REPLICAS, D, KV), 1.0, 6.0, ((0, 4), (1, 32))),
        "norm_gain": jnp.clip(1.0 + 0.15 * jax.random.normal(arg_keys[2], (REPLICAS, D), jnp.float32), 0.25, 1.75).astype(jnp.bfloat16),
        "cotangent": scatter_about(arg_keys[3], (REPLICAS, TOKENS, KV), 1.0, 6.0, ((0, 4), (1, 32))),
        "frag_global": scatter_about(arg_keys[4], (D, FRAG), 1.0, 6.0, ((0, 32),), jnp.float32),
        "frag_momentum": scatter_about(arg_keys[5], (D, FRAG), 0.5, 3.0, ((0, 32),), jnp.float32),
        "frag_snapshot": scatter_about(arg_keys[6], (REPLICAS, D, FRAG), 1.0, 6.0, ((0, 4), (1, 32))),
        "frag_local": scatter_about(arg_keys[7], (REPLICAS, D, FRAG), 1.0, 6.0, ((0, 4), (1, 32))),
    }


epsilon = 1e-05
outer_rate = 0.7
outer_beta = 0.9
merge_weight = 0.5

def inner_replica(bundle):
    tokens, weight, gain, upstream = bundle
    factor = float(D) ** (-0.5)
    wide_inputs = tokens.astype(jnp.float32)
    radius = jnp.sqrt(lax.optimization_barrier(jnp.mean(wide_inputs * wide_inputs, axis=-1, keepdims=True)) + epsilon)
    normed = wide_inputs / radius
    scaled = (normed * gain.astype(jnp.float32)[None, :]).astype(jnp.bfloat16)
    values = (factor * jnp.dot(scaled, weight, preferred_element_type=jnp.float32)).astype(jnp.bfloat16)
    adjoint = factor * jnp.dot(upstream, weight.T, preferred_element_type=jnp.float32) * gain.astype(jnp.float32)[None, :]
    correction = lax.optimization_barrier(jnp.mean(adjoint * normed, axis=-1, keepdims=True))
    input_grad = ((adjoint - normed * correction) / radius).astype(jnp.bfloat16)
    weight_grad = factor * jnp.dot(scaled.T, upstream, preferred_element_type=jnp.float32)
    return (values, input_grad, weight_grad)

def reference(layer_input, value_weight, norm_gain, cotangent, frag_global, frag_momentum, frag_snapshot, frag_local):
    values, input_grad, weight_grad = lax.map(inner_replica, (layer_input, value_weight, norm_gain, cotangent))
    deltas = frag_global[None, :, :] - frag_snapshot.astype(jnp.float32)
    mean_delta = lax.optimization_barrier(jnp.sum(deltas, axis=0)) / REPLICAS
    new_momentum = outer_beta * frag_momentum + mean_delta
    new_global = frag_global - outer_rate * (mean_delta + outer_beta * new_momentum)
    new_local = (merge_weight * frag_local.astype(jnp.float32) + (1.0 - merge_weight) * new_global[None, :, :]).astype(jnp.bfloat16)
    return (values, input_grad, weight_grad, new_global, new_momentum, new_local)
```

```python
import functools

import jax
import jax.numpy as jnp
from jax import lax
from jax.experimental import pallas as pl
from jax.experimental.pallas import tpu as pltpu
from jax.sharding import PartitionSpec as P

epsilon = 1e-05
outer_rate = 0.7
outer_beta = 0.9
merge_weight = 0.5

NZ, NX, NY = 2, 4, 4
BLOCKS = NZ * NX
MIB = 1 << 20


def _index(z, x, y):
    return (z * NX + x) * NY + y


X_GROUPS = [[_index(z, x, y) for x in range(NX)] for z in range(NZ) for y in range(NY)]
Y_GROUPS = [[_index(z, x, y) for y in range(NY)] for z in range(NZ) for x in range(NX)]
ZY_GROUPS = [[_index(z, x, y) for z in range(NZ) for y in range(NY)] for x in range(NX)]
ZX_GROUPS = [[_index(z, x, y) for z in range(NZ) for x in range(NX)] for y in range(NY)]
OTHER_CORE = [(0, 1), (1, 0), (2, 3), (3, 2)]
OTHER_Z = [(0, 2), (2, 0), (1, 3), (3, 1)]


def weight_grad_kernel(width, x_ref, cot_ref, out_ref, inv_ref, held, total, scaled):
    phase, j = pl.program_id(0), pl.program_id(1)
    tokens, cols = x_ref.shape

    @pl.when(phase == 0)
    def _():
        x = x_ref[...]
        held[j] = x
        wide = x.astype(jnp.float32)
        squares = wide * wide
        part = squares[:, :128]
        for k in range(1, cols // 128):
            part = part + squares[:, k * 128 : (k + 1) * 128]

        @pl.when(j == 0)
        def _():
            total[...] = part

        @pl.when(j > 0)
        def _():
            total[...] += part

    @pl.when(phase == 1)
    def _():
        @pl.when(j == 0)
        def _():
            mean = jnp.sum(total[...], axis=1, keepdims=True) / width
            inv = 1.0 / jnp.sqrt(mean + epsilon)
            inv_ref[...] = jnp.broadcast_to(inv, inv_ref.shape)
            scaled[...] = (cot_ref[...].astype(jnp.float32) * inv).astype(jnp.bfloat16)

        rows = cols // NY
        for y in range(NY):
            out_ref[y, 0] = lax.dot_general(
                held[j, :, y * rows : (y + 1) * rows],
                scaled[...],
                (((0,), (0,)), ((), ())),
                preferred_element_type=jnp.float32,
            ).astype(jnp.bfloat16)


def weight_grad_partial(x, cot):
    tokens, width = x.shape
    kv = cot.shape[1]
    cols = width // BLOCKS
    rows = cols // NY
    return pl.pallas_call(
        functools.partial(weight_grad_kernel, width),
        grid=(2, BLOCKS),
        in_specs=[
            pl.BlockSpec((tokens, cols), lambda p, j: (0, jnp.where(p == 0, j, BLOCKS - 1))),
            pl.BlockSpec((tokens, kv), lambda p, j: (0, 0)),
        ],
        out_specs=[
            pl.BlockSpec((NY, 1, rows, kv), lambda p, j: (0, jnp.where(p == 0, 0, j), 0, 0)),
            pl.BlockSpec((tokens, 128), lambda p, j: (0, 0)),
        ],
        out_shape=[
            jax.ShapeDtypeStruct((NY, BLOCKS, rows, kv), jnp.bfloat16),
            jax.ShapeDtypeStruct((tokens, 128), jnp.float32),
        ],
        scratch_shapes=[
            pltpu.VMEM((BLOCKS, tokens, cols), jnp.bfloat16),
            pltpu.VMEM((tokens, 128), jnp.float32),
            pltpu.VMEM((tokens, kv), jnp.bfloat16),
        ],
        compiler_params=pltpu.CompilerParams(vmem_limit_bytes=32 * MIB),
        cost_estimate=pl.CostEstimate(
            flops=2 * tokens * width * kv, bytes_accessed=4 * tokens * width, transcendentals=0
        ),
        name="weight_grad_partial",
    )(x, cot)


def input_grad_kernel(width, factor, x_ref, w_ref, cot_ref, inv_ref, val_ref, out_ref, held_x, held_w, total, shift):
    phase, j = pl.program_id(0), pl.program_id(1)

    @pl.when(phase == 0)
    def _():
        held_x[j] = x_ref[...]
        held_w[j] = w_ref[0, 0]
        part = jnp.dot(x_ref[...], w_ref[0, 0], preferred_element_type=jnp.float32)

        @pl.when(j == 0)
        def _():
            total[...] = part

        @pl.when(j > 0)
        def _():
            total[...] += part

    @pl.when(phase == 1)
    def _():
        inv = inv_ref[:, :1]

        @pl.when(j == 0)
        def _():
            values = total[...] * (factor * inv)
            val_ref[...] = values.astype(jnp.bfloat16)
            mean = jnp.sum(cot_ref[...].astype(jnp.float32) * values, axis=1, keepdims=True) / width
            shift[...] = jnp.broadcast_to(mean * inv * inv, shift.shape)

        adjoint = lax.dot_general(
            cot_ref[...], held_w[j], (((1,), (1,)), ((), ())), preferred_element_type=jnp.float32
        )
        out_ref[...] = (
            adjoint * (factor * inv) - held_x[j].astype(jnp.float32) * shift[:, :1]
        ).astype(jnp.bfloat16)


def values_and_input_grad(x, w, cot, inv):
    tokens, width = x.shape
    kv = cot.shape[1]
    cols = width // BLOCKS
    factor = float(width) ** (-0.5)
    last = BLOCKS - 1
    return pl.pallas_call(
        functools.partial(input_grad_kernel, width, factor),
        grid=(2, BLOCKS),
        in_specs=[
            pl.BlockSpec((tokens, cols), lambda p, j: (0, jnp.where(p == 0, j, last))),
            pl.BlockSpec(
                (1, 1, cols, kv),
                lambda p, j: (jnp.where(p == 0, j % NX, NX - 1), jnp.where(p == 0, j // NX, NZ - 1), 0, 0),
            ),
            pl.BlockSpec((tokens, kv), lambda p, j: (0, 0)),
            pl.BlockSpec((tokens, 128), lambda p, j: (0, 0)),
        ],
        out_specs=[
            pl.BlockSpec((tokens, kv), lambda p, j: (0, 0)),
            pl.BlockSpec((tokens, cols), lambda p, j: (0, jnp.where(p == 0, 0, j))),
        ],
        out_shape=[
            jax.ShapeDtypeStruct((tokens, kv), jnp.bfloat16),
            jax.ShapeDtypeStruct((tokens, width), jnp.bfloat16),
        ],
        scratch_shapes=[
            pltpu.VMEM((BLOCKS, tokens, cols), jnp.bfloat16),
            pltpu.VMEM((BLOCKS, cols, kv), jnp.bfloat16),
            pltpu.VMEM((tokens, kv), jnp.float32),
            pltpu.VMEM((tokens, 128), jnp.float32),
        ],
        compiler_params=pltpu.CompilerParams(vmem_limit_bytes=40 * MIB),
        cost_estimate=pl.CostEstimate(
            flops=4 * tokens * width * kv, bytes_accessed=6 * tokens * width, transcendentals=0
        ),
        name="values_and_input_grad",
    )(x, w, cot, inv)


def body(
    layer_input,
    value_weight,
    norm_gain,
    cotangent,
    frag_global,
    frag_momentum,
    frag_snapshot,
    frag_local,
):
    x = layer_input[0]
    cot = cotangent[0]
    gain = norm_gain[0].astype(jnp.float32)[:, None]
    width = x.shape[1]
    rows, kv = value_weight[0].shape
    factor = float(width) ** (-0.5)

    own = (value_weight[0].astype(jnp.float32) * gain).astype(jnp.bfloat16)
    slab = lax.all_gather(own, "fsdp", axis=0, tiled=True, axis_index_groups=ZY_GROUPS)
    weight = lax.all_gather(slab, "fsdp", axis=0, axis_index_groups=X_GROUPS)
    weight = weight.reshape(NX, NZ, NY * rows, kv)

    partial, inv = weight_grad_partial(x, cot)
    summed = lax.psum_scatter(
        partial.reshape(NY * BLOCKS * rows, kv),
        "fsdp",
        scatter_dimension=0,
        tiled=True,
        axis_index_groups=Y_GROUPS,
    )
    pieces = lax.all_to_all(
        summed.reshape(BLOCKS, rows, kv), "fsdp", 0, 0, axis_index_groups=ZX_GROUPS
    )
    weight_grad = jnp.sum(pieces.astype(jnp.float32), axis=0) * (factor * gain)

    values, input_grad = values_and_input_grad(x, weight, cot, inv)

    mine = frag_snapshot[0]
    far = lax.ppermute(mine, "rep", OTHER_Z)
    near = lax.ppermute(mine, "rep", OTHER_CORE)
    far_near = lax.ppermute(far, "rep", OTHER_CORE)
    total = (mine.astype(jnp.float32) + near.astype(jnp.float32)) + (
        far.astype(jnp.float32) + far_near.astype(jnp.float32)
    )
    mean_delta = frag_global - total * (1.0 / lax.axis_size("rep"))
    new_momentum = outer_beta * frag_momentum + mean_delta
    new_global = frag_global - outer_rate * (mean_delta + outer_beta * new_momentum)
    new_local = (
        merge_weight * frag_local[0].astype(jnp.float32) + (1.0 - merge_weight) * new_global
    ).astype(jnp.bfloat16)
    return (
        values[None],
        input_grad[None],
        weight_grad[None],
        new_global,
        new_momentum,
        new_local[None],
    )


def solution(mesh):
    return jax.shard_map(
        body,
        mesh=mesh,
        in_specs=(
            P("rep", "fsdp", None),
            P("rep", "fsdp", None),
            P("rep", "fsdp"),
            P("rep", "fsdp", None),
            P("fsdp", None),
            P("fsdp", None),
            P("rep", "fsdp", None),
            P("rep", "fsdp", None),
        ),
        out_specs=(
            P("rep", "fsdp", None),
            P("rep", "fsdp", None),
            P("rep", "fsdp", None),
            P("fsdp", None),
            P("fsdp", None),
            P("rep", "fsdp", None),
        ),
        check_vma=False,
    )
```

```python
import functools

import jax
import jax.numpy as jnp
from jax import lax
from jax.experimental import pallas as pl
from jax.experimental.pallas import tpu as pltpu
from jax.sharding import PartitionSpec as P

epsilon = 1e-05
outer_rate = 0.7
outer_beta = 0.9
merge_weight = 0.5

NZ, NX, NY = 2, 4, 4
BLOCKS = NZ * NX
MIB = 1 << 20
VMEM_LIMIT = 56 * MIB


def _index(z, x, y):
    return (z * NX + x) * NY + y


ZY_GROUPS = [[_index(z, x, y) for z in range(NZ) for y in range(NY)] for x in range(NX)]
X_GROUPS = [[_index(z, x, y) for x in range(NX)] for z in range(NZ) for y in range(NY)]


def _shift(dz, dx, dy):
    return [
        (_index(z, x, y), _index((z + dz) % NZ, (x + dx) % NX, (y + dy) % NY))
        for z in range(NZ)
        for x in range(NX)
        for y in range(NY)
    ]


Z_SWAP = _shift(1, 0, 0)
X_UP, X_DOWN = _shift(0, 1, 0), _shift(0, -1, 0)
Y_UP, Y_DOWN = _shift(0, 0, 1), _shift(0, 0, -1)
MIB = 1 << 20
VMEM_LIMIT = 56 * MIB


def _index(z, x, y):
    return (z * NX + x) * NY + y


ZY_GROUPS = [[_index(z, x, y) for z in range(NZ) for y in range(NY)] for x in range(NX)]
ZX_GROUPS = [[_index(z, x, y) for z in range(NZ) for x in range(NX)] for y in range(NY)]


def _shift(dz, dx, dy):
    return [
        (_index(z, x, y), _index((z + dz) % NZ, (x + dx) % NX, (y + dy) % NY))
        for z in range(NZ)
        for x in range(NX)
        for y in range(NY)
    ]


Z_SWAP = _shift(1, 0, 0)
X_UP, X_DOWN = _shift(0, 1, 0), _shift(0, -1, 0)
Y_UP, Y_DOWN = _shift(0, 0, 1), _shift(0, 0, -1)
OTHER_CORE = [(0, 1), (1, 0), (2, 3), (3, 2)]
OTHER_Z = [(0, 2), (2, 0), (1, 3), (3, 1)]


HBM = pl.BlockSpec(memory_space=pl.ANY)
VMEM = pl.BlockSpec(memory_space=pltpu.VMEM)
SMEM = pl.BlockSpec(memory_space=pltpu.SMEM)
CHUNKS = 8

FIRST = ((2, 0), (1, 1), (2, 1), (NX - 1, 0))
REST = ((1, 0), (NX - 1, 1), (0, 0), (0, 1))


def norm_kernel(width, x_ref, cot_ref, inv_ref, scaled_ref, held, sems):
    chunks, rows = held.shape[:2]

    def copy(k):
        return pltpu.make_async_copy(x_ref.at[pl.ds(k * rows, rows)], held.at[k], sems.at[k])

    for k in range(chunks):
        copy(k).start()
    for k in range(chunks):
        copy(k).wait()

        def add(c, total):
            wide = held[k, :, pl.ds(pl.multiple_of(c * 512, 512), 512)].astype(jnp.float32)
            squares = wide * wide
            return (
                total
                + (squares[:, :128] + squares[:, 128:256])
                + (squares[:, 256:384] + squares[:, 384:])
            )

        total = lax.fori_loop(0, width // 512, add, jnp.zeros((rows, 128), jnp.float32), unroll=4)
        inv = 1.0 / jnp.sqrt(jnp.sum(total, axis=1, keepdims=True) / width + epsilon)
        here = pl.ds(k * rows, rows)
        inv_ref[here, :] = jnp.broadcast_to(inv, (rows, 128))
        scaled_ref[here, :] = (cot_ref[here, :].astype(jnp.float32) * inv).astype(jnp.bfloat16)


def norm_and_scaled_cotangent(x, cot):
    tokens, width = x.shape
    kv = cot.shape[1]
    return pl.pallas_call(
        functools.partial(norm_kernel, width),
        in_specs=[HBM, VMEM],
        out_specs=[VMEM, VMEM],
        out_shape=[
            jax.ShapeDtypeStruct((tokens, 128), jnp.float32),
            jax.ShapeDtypeStruct((tokens, kv), jnp.bfloat16),
        ],
        scratch_shapes=[
            pltpu.VMEM((CHUNKS, tokens // CHUNKS, width), jnp.bfloat16),
            pltpu.SemaphoreType.DMA((CHUNKS,)),
        ],
        compiler_params=pltpu.CompilerParams(vmem_limit_bytes=VMEM_LIMIT),
        cost_estimate=pl.CostEstimate(
            flops=8 * tokens * width, bytes_accessed=2 * tokens * width, transcendentals=0
        ),
        name="norm_and_scaled_cotangent",
    )(x, cot)


def weight_grad_kernel(todo, place_ref, x_ref, scaled_ref, *rest):
    outs, (held, stage, load_sems, store_sems) = rest[:4], rest[4:]
    cols = held.shape[2]
    rows = cols // NY // 2
    x = place_ref[0]

    def load(k):
        d, z = todo[k]
        j = z * NX + lax.rem(x + d, NX)
        columns = pl.ds(pl.multiple_of(j * cols, cols), cols)
        return pltpu.make_async_copy(x_ref.at[:, columns], held.at[k], load_sems.at[k])

    def store(half, k):
        n = half * len(todo) + k
        where = outs[n // 2].at[pl.ds((n % 2) * NY * rows, NY * rows)]
        return pltpu.make_async_copy(stage.at[n], where, store_sems.at[n])

    for k in range(len(todo)):
        load(k).start()
    for k in range(len(todo)):
        load(k).wait()
        for half in (0, 1):
            for p in range(NY):
                stage[half * len(todo) + k, p * rows : (p + 1) * rows, :] = lax.dot_general(
                    held[k, :, (2 * p + half) * rows : (2 * p + half + 1) * rows],
                    scaled_ref[...],
                    (((0,), (0,)), ((), ())),
                    preferred_element_type=jnp.float32,
                ).astype(stage.dtype)
            store(half, k).start()
    for k in range(len(todo)):
        for half in (0, 1):
            store(half, k).wait()


def weight_grad_chunks(x, scaled, place, todo, dtype):
    tokens, width = x.shape
    kv = scaled.shape[1]
    cols = width // BLOCKS
    rows = cols // NY // 2
    return pl.pallas_call(
        functools.partial(weight_grad_kernel, todo),
        in_specs=[SMEM, HBM, VMEM],
        out_specs=[HBM] * 4,
        out_shape=[jax.ShapeDtypeStruct((2 * NY * rows, kv), dtype)] * 4,
        scratch_shapes=[
            pltpu.VMEM((len(todo), tokens, cols), jnp.bfloat16),
            pltpu.VMEM((2 * len(todo), NY * rows, kv), dtype),
            pltpu.SemaphoreType.DMA((len(todo),)),
            pltpu.SemaphoreType.DMA((2 * len(todo),)),
        ],
        compiler_params=pltpu.CompilerParams(vmem_limit_bytes=VMEM_LIMIT),
        cost_estimate=pl.CostEstimate(
            flops=tokens * width * kv, bytes_accessed=2 * tokens * width, transcendentals=0
        ),
        name="weight_grad_chunks",
    )(place, x, scaled)


def assemble_kernel(plan, rows_in, *refs):
    arrays, refs = refs[: len(rows_in)], refs[len(rows_in) :]
    outs, refs = refs[: len(plan)], refs[len(plan) :]
    stages, refs = refs[: len(plan)], refs[len(plan) :]
    *held, load_sems, store_sems = refs

    loads = []
    n = taken = 0
    for stage, segments in zip(stages, plan):
        start = 0
        for rows, sources in segments:
            here = []
            for array, first in sources:
                if len(sources) == 1:
                    target = stage.at[pl.ds(start, rows)]
                else:
                    target = held[taken]
                    taken += 1
                source = arrays[array].at[pl.ds(first, rows)]
                here.append((pltpu.make_async_copy(source, target, load_sems.at[n]), target))
                n += 1
            loads.append(here)
            start += rows
    for here in loads:
        for copy, _ in here:
            copy.start()
    stores = []
    k = 0
    for m, (out, stage, segments) in enumerate(zip(outs, stages, plan)):
        start = 0
        for rows, sources in segments:
            here = loads[k]
            k += 1
            for copy, _ in here:
                copy.wait()
            if len(sources) > 1:
                total = here[0][1][...].astype(jnp.float32)
                for _, target in here[1:]:
                    total = total + target[...].astype(jnp.float32)
                stage[start : start + rows, :] = total.astype(stage.dtype)
            start += rows
        stores.append(pltpu.make_async_copy(stage, out, store_sems.at[m]))
        stores[-1].start()
    for store in stores:
        store.wait()


def assemble(arrays, plan):
    kv = arrays[0].shape[1]
    sizes = [sum(rows for rows, _ in segments) for segments in plan]
    held = [
        pltpu.VMEM((rows, kv), arrays[array].dtype)
        for segments in plan
        for rows, sources in segments
        if len(sources) > 1
        for array, _ in sources
    ]
    copies = sum(len(sources) for segments in plan for _, sources in segments)
    return pl.pallas_call(
        functools.partial(assemble_kernel, plan, [a.shape[0] for a in arrays]),
        in_specs=[HBM] * len(arrays),
        out_specs=[HBM] * len(plan),
        out_shape=[jax.ShapeDtypeStruct((size, kv), jnp.bfloat16) for size in sizes],
        scratch_shapes=[pltpu.VMEM((size, kv), jnp.bfloat16) for size in sizes]
        + held
        + [pltpu.SemaphoreType.DMA((copies,)), pltpu.SemaphoreType.DMA((len(plan),))],
        compiler_params=pltpu.CompilerParams(vmem_limit_bytes=VMEM_LIMIT),
        cost_estimate=pl.CostEstimate(
            flops=sum(sizes) * kv, bytes_accessed=6 * sum(sizes) * kv, transcendentals=0
        ),
        name="assemble",
    )(*arrays)


def strip_copy(x_ref, strips, sems, owners_ref, k):
    rows = strips.shape[2]
    columns = pl.ds(pl.multiple_of(owners_ref[k] * rows, rows), rows)
    return pltpu.make_async_copy(x_ref.at[:, columns], strips.at[k], sems.at[k])


def projection_kernel(count, owners_ref, x_ref, *rest):
    *refs, total_ref, strips, held_w, w_sems, x_sems = rest
    rows = strips.shape[2]
    per_array = count // len(refs)

    def weight(k):
        block = refs[k // per_array].at[pl.ds((k % per_array) * rows, rows)]
        return pltpu.make_async_copy(block, held_w.at[k], w_sems.at[k])

    for k in range(count):
        strip_copy(x_ref, strips, x_sems, owners_ref, k).start()
        weight(k).start()
    for k in range(count):
        strip_copy(x_ref, strips, x_sems, owners_ref, k).wait()
        weight(k).wait()
        part = jnp.dot(strips[k], held_w[k], preferred_element_type=jnp.float32)
        total_ref[...] = part if k == 0 else total_ref[...] + part


def projection(x, arrays, owners):
    tokens, width = x.shape
    kv = arrays[0].shape[1]
    rows = width // BLOCKS // NY
    count = NX * len(arrays)
    return pl.pallas_call(
        functools.partial(projection_kernel, count),
        in_specs=[SMEM, HBM] + [HBM] * len(arrays),
        out_specs=VMEM,
        out_shape=jax.ShapeDtypeStruct((tokens, kv), jnp.float32),
        scratch_shapes=[
            pltpu.VMEM((count, tokens, rows), jnp.bfloat16),
            pltpu.VMEM((count, rows, kv), jnp.bfloat16),
            pltpu.SemaphoreType.DMA((count,)),
            pltpu.SemaphoreType.DMA((count,)),
        ],
        compiler_params=pltpu.CompilerParams(vmem_limit_bytes=VMEM_LIMIT),
        cost_estimate=pl.CostEstimate(
            flops=2 * tokens * rows * count * kv,
            bytes_accessed=4 * tokens * rows * count,
            transcendentals=0,
        ),
        name="projection",
    )(owners, x, *arrays)


def input_grad_kernel(width, factor, late, owners_ref, x_ref, cot_ref, inv_ref, total_ref, *rest):
    *refs, val_ref, out_ref, held_x, held_w, strips, stage, w_sems, x_sems, strip_sems, out_sems = rest
    tokens, cols = held_x.shape[1:]
    rows, kv = held_w.shape[1:]
    first = BLOCKS * NY - late
    per_side = len(refs) // NZ

    def weight(side, n, k):
        array = side * per_side + n
        y = lax.rem(owners_ref[array * NX], NY)
        where = held_w.at[(side * NX + k) * NY + y]
        return pltpu.make_async_copy(
            refs[array].at[pl.ds(k * rows, rows)], where, w_sems.at[array * NX + k]
        )

    def columns(ref, held, sems, side, k, out):
        j = owners_ref[side * per_side * NX + k] // NY
        where = ref.at[:, pl.ds(pl.multiple_of(j * cols, cols), cols)]
        step = side * NX + k
        if out:
            return pltpu.make_async_copy(held.at[step], where, sems.at[step])
        return pltpu.make_async_copy(where, held.at[step], sems.at[step])

    def strip(side, k):
        n = side * NX + k
        owner = owners_ref[(side * per_side + per_side - 1) * NX + k]
        where = x_ref.at[:, pl.ds(pl.multiple_of(owner * rows, rows), rows)]
        return pltpu.make_async_copy(where, strips.at[n], strip_sems.at[n])

    steps = [(side, k) for side in range(NZ) for k in range(NX)]
    for side, k in steps:
        strip(side, k).start()
        weight(side, per_side - 1, k).start()
    for side, k in steps:
        for n in range(per_side - 1):
            weight(side, n, k).start()
        columns(x_ref, held_x, x_sems, side, k, False).start()
    total = total_ref[...]
    for side, k in steps:
        strip(side, k).wait()
        weight(side, per_side - 1, k).wait()
        y = lax.rem(owners_ref[(side * per_side + per_side - 1) * NX], NY)
        total = total + jnp.dot(
            strips[side * NX + k],
            held_w[(side * NX + k) * NY + y],
            preferred_element_type=jnp.float32,
        )
    inv = inv_ref[:, :1]
    values = total * (factor * inv)
    val_ref[...] = values.astype(jnp.bfloat16)
    mean = jnp.sum(cot_ref[...].astype(jnp.float32) * values, axis=1, keepdims=True) / width
    shift = mean * inv * inv
    scale = factor * inv

    for side, k in steps:
        for n in range(per_side - 1):
            weight(side, n, k).wait()
        columns(x_ref, held_x, x_sems, side, k, False).wait()
        step = side * NX + k
        for n in range(NY):
            adjoint = lax.dot_general(
                cot_ref[...],
                held_w[step * NY + n],
                (((1,), (1,)), ((), ())),
                preferred_element_type=jnp.float32,
            )
            here = slice(n * rows, (n + 1) * rows)
            stage[step, :, here] = (
                adjoint * scale - held_x[step, :, here].astype(jnp.float32) * shift
            ).astype(jnp.bfloat16)
        columns(out_ref, stage, out_sems, side, k, True).start()
    for side, k in steps:
        columns(out_ref, stage, out_sems, side, k, True).wait()


def values_and_input_grad(x, arrays, owners, total, cot, inv):
    late = NZ * NX
    tokens, width = x.shape
    kv = cot.shape[1]
    cols = width // BLOCKS
    rows = cols // NY
    factor = float(width) ** (-0.5)
    return pl.pallas_call(
        functools.partial(input_grad_kernel, width, factor, late),
        in_specs=[SMEM, HBM, VMEM, VMEM, VMEM] + [HBM] * len(arrays),
        out_specs=[VMEM, HBM],
        out_shape=[
            jax.ShapeDtypeStruct((tokens, kv), jnp.bfloat16),
            jax.ShapeDtypeStruct((tokens, width), jnp.bfloat16),
        ],
        scratch_shapes=[
            pltpu.VMEM((BLOCKS, tokens, cols), jnp.bfloat16),
            pltpu.VMEM((BLOCKS * NY, rows, kv), jnp.bfloat16),
            pltpu.VMEM((late, tokens, rows), jnp.bfloat16),
            pltpu.VMEM((BLOCKS, tokens, cols), jnp.bfloat16),
            pltpu.SemaphoreType.DMA((BLOCKS * NY,)),
            pltpu.SemaphoreType.DMA((BLOCKS,)),
            pltpu.SemaphoreType.DMA((late,)),
            pltpu.SemaphoreType.DMA((BLOCKS,)),
        ],
        compiler_params=pltpu.CompilerParams(vmem_limit_bytes=VMEM_LIMIT),
        cost_estimate=pl.CostEstimate(
            flops=2 * tokens * width * kv, bytes_accessed=6 * tokens * width, transcendentals=0
        ),
        name="values_and_input_grad",
    )(owners, x, cot, inv, total, *arrays)


def send(block, where):
    return lax.ppermute(block, "fsdp", where)


def block_order(z, y):
    places = [(dz, dy) for dz in (0, 1) for dy in (0, -1, 1)] + [(0, 2), (1, 2)]
    return jnp.stack(
        [_index((z + dz) % NZ, k, (y + dy) % NY) for dz, dy in places for k in range(NX)]
    ).astype(jnp.int32)


def final_order(owners):
    near, others, far = owners[: 3 * NX], owners[3 * NX : 6 * NX], owners[6 * NX :]
    return jnp.concatenate([near, far[:NX], others, far[NX:]])


def body(
    layer_input,
    value_weight,
    norm_gain,
    cotangent,
    frag_global,
    frag_momentum,
    frag_snapshot,
    frag_local,
):
    x = layer_input[0]
    cot = cotangent[0]
    gain = norm_gain[0].astype(jnp.float32)[:, None]
    width = x.shape[1]
    rows, kv = value_weight[0].shape
    half = rows // 2
    factor = float(width) ** (-0.5)
    me = lax.axis_index("fsdp")
    place = jnp.reshape((me // NY) % NX, (1,)).astype(jnp.int32)
    f32 = jnp.float32

    def after(values, *others):
        return lax.optimization_barrier((values, others))[0]

    own = (value_weight[0].astype(f32) * gain).astype(jnp.bfloat16)
    slab = lax.all_to_all(
        jnp.broadcast_to(own, (NX, rows, kv)), "fsdp", 0, 0, axis_index_groups=X_GROUPS
    ).reshape(NX * rows, kv)
    inv, scaled = norm_and_scaled_cotangent(x, cot)

    chunk = NY * half
    sent = weight_grad_chunks(x, scaled, place, FIRST, jnp.bfloat16)
    got = [[send(sent[0], X_UP), send(sent[1], X_DOWN)]]
    below, above, other = send(slab, Y_UP), send(slab, Y_DOWN), send(slab, Z_SWAP)

    first = (got[0], below, above, other)
    messages = after(sent[2:], got[0])
    got.append([send(m, r) for m, r in zip(messages, (X_UP, X_DOWN))])
    message = after(other, below, above)
    other_below, other_above = send(message, Y_UP), send(message, Y_DOWN)

    owners = block_order(me // (NX * NY), me % NY)
    near, others = [slab, below, above], [other, other_below, other_above]
    kept = weight_grad_chunks(x, scaled, place, REST, f32)
    add = [[(chunk, [(0, way * chunk), (1 + way, 0)])] for way in (0, 1)]
    messages = after(assemble([kept[0], *got[0]], add), got[1])
    then = [[send(m, r) for m, r in zip(messages, (X_UP, X_DOWN))]]
    messages = after([below, other_above], other_below)
    far = [send(messages[0], Y_UP), send(messages[1], Y_DOWN)]
    messages = after(assemble([kept[2], *got[1]], add), then[0])
    then.append([send(m, r) for m, r in zip(messages, (X_UP, X_DOWN))])

    mine = after(frag_snapshot[0], *first)
    everyone = jnp.broadcast_to(mine, (lax.axis_size("rep"), *mine.shape))
    total = jnp.sum(lax.all_to_all(everyone, "rep", 0, 0).astype(f32), axis=0)
    mean_delta = frag_global - total * (1.0 / lax.axis_size("rep"))
    new_momentum = outer_beta * frag_momentum + mean_delta
    new_global = frag_global - outer_rate * (mean_delta + outer_beta * new_momentum)
    new_local = (
        merge_weight * frag_local[0].astype(f32) + (1.0 - merge_weight) * new_global
    ).astype(jnp.bfloat16)

    product = projection(x, [*near, *others], owners)

    arrays = [kept[1], *got[0], *then[0], kept[3], *got[1], *then[1]]
    segments = []
    for k in range(BLOCKS):
        z, start = k // NY, k % NY * half
        for n in (0, 5):
            came = [(n + 2 - z, chunk + start), (n + 3 + z, start)]
            segments.append((half, [(n, k * half), *came]))
    (ring,) = assemble(after(arrays, far, product, new_local), [segments])
    group = lax.all_to_all(ring.reshape(BLOCKS, rows, kv), "fsdp", 0, 0, axis_index_groups=ZY_GROUPS)

    values, input_grad = values_and_input_grad(
        x, [*near, far[0], *others, far[1]], final_order(owners), product, cot, inv
    )
    group = after(group, input_grad)
    weight_grad = jnp.sum(group.astype(f32), axis=0) * (factor * gain)
    return (
        values[None],
        input_grad[None],
        weight_grad[None],
        new_global,
        new_momentum,
        new_local[None],
    )


def solution(mesh):
    return jax.shard_map(
        body,
        mesh=mesh,
        in_specs=(
            P("rep", "fsdp", None),
            P("rep", "fsdp", None),
            P("rep", "fsdp"),
            P("rep", "fsdp", None),
            P("fsdp", None),
            P("fsdp", None),
            P("rep", "fsdp", None),
            P("rep", "fsdp", None),
        ),
        out_specs=(
            P("rep", "fsdp", None),
            P("rep", "fsdp", None),
            P("rep", "fsdp", None),
            P("fsdp", None),
            P("fsdp", None),
            P("rep", "fsdp", None),
        ),
        check_vma=False,
    )
```

```python
import functools

import jax
import jax.numpy as jnp
from jax import lax
from jax.experimental import pallas as pl
from jax.experimental.pallas import tpu as pltpu
from jax.sharding import PartitionSpec as P

epsilon = 1e-05
outer_rate = 0.7
outer_beta = 0.9
merge_weight = 0.5

NZ, NX, NY = 2, 4, 4
BLOCKS = NZ * NX
MIB = 1 << 20
VMEM_LIMIT = 56 * MIB


def _index(z, x, y):
    return (z * NX + x) * NY + y


ZY_GROUPS = [[_index(z, x, y) for z in range(NZ) for y in range(NY)] for x in range(NX)]
X_GROUPS = [[_index(z, x, y) for x in range(NX)] for z in range(NZ) for y in range(NY)]


def _shift(dz, dx, dy):
    return [
        (_index(z, x, y), _index((z + dz) % NZ, (x + dx) % NX, (y + dy) % NY))
        for z in range(NZ)
        for x in range(NX)
        for y in range(NY)
    ]


Z_SWAP = _shift(1, 0, 0)
X_UP, X_DOWN = _shift(0, 1, 0), _shift(0, -1, 0)
Y_UP, Y_DOWN = _shift(0, 0, 1), _shift(0, 0, -1)
MIB = 1 << 20
VMEM_LIMIT = 56 * MIB


def _index(z, x, y):
    return (z * NX + x) * NY + y


ZY_GROUPS = [[_index(z, x, y) for z in range(NZ) for y in range(NY)] for x in range(NX)]
ZX_GROUPS = [[_index(z, x, y) for z in range(NZ) for x in range(NX)] for y in range(NY)]


def _shift(dz, dx, dy):
    return [
        (_index(z, x, y), _index((z + dz) % NZ, (x + dx) % NX, (y + dy) % NY))
        for z in range(NZ)
        for x in range(NX)
        for y in range(NY)
    ]


Z_SWAP = _shift(1, 0, 0)
X_UP, X_DOWN = _shift(0, 1, 0), _shift(0, -1, 0)
Y_UP, Y_DOWN = _shift(0, 0, 1), _shift(0, 0, -1)
OTHER_CORE = [(0, 1), (1, 0), (2, 3), (3, 2)]
OTHER_Z = [(0, 2), (2, 0), (1, 3), (3, 1)]


HBM = pl.BlockSpec(memory_space=pl.ANY)
VMEM = pl.BlockSpec(memory_space=pltpu.VMEM)
SMEM = pl.BlockSpec(memory_space=pltpu.SMEM)
CHUNKS = 8

FIRST = ((2, 0), (1, 1), (2, 1), (NX - 1, 0))
REST = ((1, 0), (NX - 1, 1), (0, 0), (0, 1))


def norm_kernel(width, x_ref, cot_ref, inv_ref, scaled_ref, held, sems):
    chunks, rows = held.shape[:2]

    def copy(k):
        return pltpu.make_async_copy(x_ref.at[pl.ds(k * rows, rows)], held.at[k], sems.at[k])

    for k in range(chunks):
        copy(k).start()
    for k in range(chunks):
        copy(k).wait()

        def add(c, total):
            wide = held[k, :, pl.ds(pl.multiple_of(c * 512, 512), 512)].astype(jnp.float32)
            squares = wide * wide
            return (
                total
                + (squares[:, :128] + squares[:, 128:256])
                + (squares[:, 256:384] + squares[:, 384:])
            )

        total = lax.fori_loop(0, width // 512, add, jnp.zeros((rows, 128), jnp.float32), unroll=4)
        inv = 1.0 / jnp.sqrt(jnp.sum(total, axis=1, keepdims=True) / width + epsilon)
        here = pl.ds(k * rows, rows)
        inv_ref[here, :] = jnp.broadcast_to(inv, (rows, 128))
        scaled_ref[here, :] = (cot_ref[here, :].astype(jnp.float32) * inv).astype(jnp.bfloat16)


def norm_and_scaled_cotangent(x, cot):
    tokens, width = x.shape
    kv = cot.shape[1]
    return pl.pallas_call(
        functools.partial(norm_kernel, width),
        in_specs=[HBM, VMEM],
        out_specs=[VMEM, VMEM],
        out_shape=[
            jax.ShapeDtypeStruct((tokens, 128), jnp.float32),
            jax.ShapeDtypeStruct((tokens, kv), jnp.bfloat16),
        ],
        scratch_shapes=[
            pltpu.VMEM((CHUNKS, tokens // CHUNKS, width), jnp.bfloat16),
            pltpu.SemaphoreType.DMA((CHUNKS,)),
        ],
        compiler_params=pltpu.CompilerParams(vmem_limit_bytes=VMEM_LIMIT),
        cost_estimate=pl.CostEstimate(
            flops=8 * tokens * width, bytes_accessed=2 * tokens * width, transcendentals=0
        ),
        name="norm_and_scaled_cotangent",
    )(x, cot)


def weight_grad_kernel(todo, place_ref, x_ref, scaled_ref, *rest):
    outs, (held, stage, load_sems, store_sems) = rest[:4], rest[4:]
    cols = held.shape[2]
    rows = cols // NY // 2
    x = place_ref[0]

    def load(k):
        d, z = todo[k]
        j = z * NX + lax.rem(x + d, NX)
        columns = pl.ds(pl.multiple_of(j * cols, cols), cols)
        return pltpu.make_async_copy(x_ref.at[:, columns], held.at[k], load_sems.at[k])

    def store(half, k):
        n = half * len(todo) + k
        where = outs[n // 2].at[pl.ds((n % 2) * NY * rows, NY * rows)]
        return pltpu.make_async_copy(stage.at[n], where, store_sems.at[n])

    for k in range(len(todo)):
        load(k).start()
    for k in range(len(todo)):
        load(k).wait()
        for half in (0, 1):
            for p in range(NY):
                stage[half * len(todo) + k, p * rows : (p + 1) * rows, :] = lax.dot_general(
                    held[k, :, (2 * p + half) * rows : (2 * p + half + 1) * rows],
                    scaled_ref[...],
                    (((0,), (0,)), ((), ())),
                    preferred_element_type=jnp.float32,
                ).astype(stage.dtype)
            store(half, k).start()
    for k in range(len(todo)):
        for half in (0, 1):
            store(half, k).wait()


def weight_grad_chunks(x, scaled, place, todo, dtype):
    tokens, width = x.shape
    kv = scaled.shape[1]
    cols = width // BLOCKS
    rows = cols // NY // 2
    return pl.pallas_call(
        functools.partial(weight_grad_kernel, todo),
        in_specs=[SMEM, HBM, VMEM],
        out_specs=[HBM] * 4,
        out_shape=[jax.ShapeDtypeStruct((2 * NY * rows, kv), dtype)] * 4,
        scratch_shapes=[
            pltpu.VMEM((len(todo), tokens, cols), jnp.bfloat16),
            pltpu.VMEM((2 * len(todo), NY * rows, kv), dtype),
            pltpu.SemaphoreType.DMA((len(todo),)),
            pltpu.SemaphoreType.DMA((2 * len(todo),)),
        ],
        compiler_params=pltpu.CompilerParams(vmem_limit_bytes=VMEM_LIMIT),
        cost_estimate=pl.CostEstimate(
            flops=tokens * width * kv, bytes_accessed=2 * tokens * width, transcendentals=0
        ),
        name="weight_grad_chunks",
    )(place, x, scaled)


def assemble_kernel(plan, rows_in, *refs):
    arrays, refs = refs[: len(rows_in)], refs[len(rows_in) :]
    outs, refs = refs[: len(plan)], refs[len(plan) :]
    stages, refs = refs[: len(plan)], refs[len(plan) :]
    *held, load_sems, store_sems = refs

    loads = []
    n = taken = 0
    for stage, segments in zip(stages, plan):
        start = 0
        for rows, sources in segments:
            here = []
            for array, first in sources:
                if len(sources) == 1:
                    target = stage.at[pl.ds(start, rows)]
                else:
                    target = held[taken]
                    taken += 1
                source = arrays[array].at[pl.ds(first, rows)]
                here.append((pltpu.make_async_copy(source, target, load_sems.at[n]), target))
                n += 1
            loads.append(here)
            start += rows
    for here in loads:
        for copy, _ in here:
            copy.start()
    stores = []
    k = 0
    for m, (out, stage, segments) in enumerate(zip(outs, stages, plan)):
        start = 0
        for rows, sources in segments:
            here = loads[k]
            k += 1
            for copy, _ in here:
                copy.wait()
            if len(sources) > 1:
                total = here[0][1][...].astype(jnp.float32)
                for _, target in here[1:]:
                    total = total + target[...].astype(jnp.float32)
                stage[start : start + rows, :] = total.astype(stage.dtype)
            start += rows
        stores.append(pltpu.make_async_copy(stage, out, store_sems.at[m]))
        stores[-1].start()
    for store in stores:
        store.wait()


def assemble(arrays, plan):
    kv = arrays[0].shape[1]
    sizes = [sum(rows for rows, _ in segments) for segments in plan]
    held = [
        pltpu.VMEM((rows, kv), arrays[array].dtype)
        for segments in plan
        for rows, sources in segments
        if len(sources) > 1
        for array, _ in sources
    ]
    copies = sum(len(sources) for segments in plan for _, sources in segments)
    return pl.pallas_call(
        functools.partial(assemble_kernel, plan, [a.shape[0] for a in arrays]),
        in_specs=[HBM] * len(arrays),
        out_specs=[HBM] * len(plan),
        out_shape=[jax.ShapeDtypeStruct((size, kv), jnp.bfloat16) for size in sizes],
        scratch_shapes=[pltpu.VMEM((size, kv), jnp.bfloat16) for size in sizes]
        + held
        + [pltpu.SemaphoreType.DMA((copies,)), pltpu.SemaphoreType.DMA((len(plan),))],
        compiler_params=pltpu.CompilerParams(vmem_limit_bytes=VMEM_LIMIT),
        cost_estimate=pl.CostEstimate(
            flops=sum(sizes) * kv, bytes_accessed=6 * sum(sizes) * kv, transcendentals=0
        ),
        name="assemble",
    )(*arrays)


def strip_copy(x_ref, strips, sems, owners_ref, k):
    rows = strips.shape[2]
    columns = pl.ds(pl.multiple_of(owners_ref[k] * rows, rows), rows)
    return pltpu.make_async_copy(x_ref.at[:, columns], strips.at[k], sems.at[k])


def projection_kernel(count, owners_ref, x_ref, *rest):
    *refs, total_ref, strips, held_w, w_sems, x_sems = rest
    rows = strips.shape[2]
    per_array = count // len(refs)

    def weight(k):
        block = refs[k // per_array].at[pl.ds((k % per_array) * rows, rows)]
        return pltpu.make_async_copy(block, held_w.at[k], w_sems.at[k])

    for k in range(count):
        strip_copy(x_ref, strips, x_sems, owners_ref, k).start()
        weight(k).start()
    for k in range(count):
        strip_copy(x_ref, strips, x_sems, owners_ref, k).wait()
        weight(k).wait()
        part = jnp.dot(strips[k], held_w[k], preferred_element_type=jnp.float32)
        total_ref[...] = part if k == 0 else total_ref[...] + part


def projection(x, arrays, owners):
    tokens, width = x.shape
    kv = arrays[0].shape[1]
    rows = width // BLOCKS // NY
    count = NX * len(arrays)
    return pl.pallas_call(
        functools.partial(projection_kernel, count),
        in_specs=[SMEM, HBM] + [HBM] * len(arrays),
        out_specs=VMEM,
        out_shape=jax.ShapeDtypeStruct((tokens, kv), jnp.float32),
        scratch_shapes=[
            pltpu.VMEM((count, tokens, rows), jnp.bfloat16),
            pltpu.VMEM((count, rows, kv), jnp.bfloat16),
            pltpu.SemaphoreType.DMA((count,)),
            pltpu.SemaphoreType.DMA((count,)),
        ],
        compiler_params=pltpu.CompilerParams(vmem_limit_bytes=VMEM_LIMIT),
        cost_estimate=pl.CostEstimate(
            flops=2 * tokens * rows * count * kv,
            bytes_accessed=4 * tokens * rows * count,
            transcendentals=0,
        ),
        name="projection",
    )(owners, x, *arrays)


def input_grad_kernel(width, factor, late, owners_ref, x_ref, cot_ref, inv_ref, total_ref, *rest):
    *refs, val_ref, out_ref, held_x, held_w, strips, stage, w_sems, x_sems, strip_sems, out_sems = rest
    tokens, cols = held_x.shape[1:]
    rows, kv = held_w.shape[1:]
    first = BLOCKS * NY - late
    per_side = len(refs) // NZ

    def weight(side, n, k):
        array = side * per_side + n
        y = lax.rem(owners_ref[array * NX], NY)
        where = held_w.at[(side * NX + k) * NY + y]
        return pltpu.make_async_copy(
            refs[array].at[pl.ds(k * rows, rows)], where, w_sems.at[array * NX + k]
        )

    def columns(ref, held, sems, side, k, out):
        j = owners_ref[side * per_side * NX + k] // NY
        where = ref.at[:, pl.ds(pl.multiple_of(j * cols, cols), cols)]
        step = side * NX + k
        if out:
            return pltpu.make_async_copy(held.at[step], where, sems.at[step])
        return pltpu.make_async_copy(where, held.at[step], sems.at[step])

    def strip(side, k):
        n = side * NX + k
        owner = owners_ref[(side * per_side + per_side - 1) * NX + k]
        where = x_ref.at[:, pl.ds(pl.multiple_of(owner * rows, rows), rows)]
        return pltpu.make_async_copy(where, strips.at[n], strip_sems.at[n])

    steps = [(side, k) for side in range(NZ) for k in range(NX)]
    for side, k in steps:
        strip(side, k).start()
        weight(side, per_side - 1, k).start()
    for side, k in steps:
        for n in range(per_side - 1):
            weight(side, n, k).start()
        columns(x_ref, held_x, x_sems, side, k, False).start()
    total = total_ref[...]
    for side, k in steps:
        strip(side, k).wait()
        weight(side, per_side - 1, k).wait()
        y = lax.rem(owners_ref[(side * per_side + per_side - 1) * NX], NY)
        total = total + jnp.dot(
            strips[side * NX + k],
            held_w[(side * NX + k) * NY + y],
            preferred_element_type=jnp.float32,
        )
    inv = inv_ref[:, :1]
    values = total * (factor * inv)
    val_ref[...] = values.astype(jnp.bfloat16)
    mean = jnp.sum(cot_ref[...].astype(jnp.float32) * values, axis=1, keepdims=True) / width
    shift = mean * inv * inv
    scale = factor * inv

    for side, k in steps:
        for n in range(per_side - 1):
            weight(side, n, k).wait()
        columns(x_ref, held_x, x_sems, side, k, False).wait()
        step = side * NX + k
        for n in range(NY):
            adjoint = lax.dot_general(
                cot_ref[...],
                held_w[step * NY + n],
                (((1,), (1,)), ((), ())),
                preferred_element_type=jnp.float32,
            )
            here = slice(n * rows, (n + 1) * rows)
            stage[step, :, here] = (
                adjoint * scale - held_x[step, :, here].astype(jnp.float32) * shift
            ).astype(jnp.bfloat16)
        columns(out_ref, stage, out_sems, side, k, True).start()
    for side, k in steps:
        columns(out_ref, stage, out_sems, side, k, True).wait()


def values_and_input_grad(x, arrays, owners, total, cot, inv):
    late = NZ * NX
    tokens, width = x.shape
    kv = cot.shape[1]
    cols = width // BLOCKS
    rows = cols // NY
    factor = float(width) ** (-0.5)
    return pl.pallas_call(
        functools.partial(input_grad_kernel, width, factor, late),
        in_specs=[SMEM, HBM, VMEM, VMEM, VMEM] + [HBM] * len(arrays),
        out_specs=[VMEM, HBM],
        out_shape=[
            jax.ShapeDtypeStruct((tokens, kv), jnp.bfloat16),
            jax.ShapeDtypeStruct((tokens, width), jnp.bfloat16),
        ],
        scratch_shapes=[
            pltpu.VMEM((BLOCKS, tokens, cols), jnp.bfloat16),
            pltpu.VMEM((BLOCKS * NY, rows, kv), jnp.bfloat16),
            pltpu.VMEM((late, tokens, rows), jnp.bfloat16),
            pltpu.VMEM((BLOCKS, tokens, cols), jnp.bfloat16),
            pltpu.SemaphoreType.DMA((BLOCKS * NY,)),
            pltpu.SemaphoreType.DMA((BLOCKS,)),
            pltpu.SemaphoreType.DMA((late,)),
            pltpu.SemaphoreType.DMA((BLOCKS,)),
        ],
        compiler_params=pltpu.CompilerParams(vmem_limit_bytes=VMEM_LIMIT),
        cost_estimate=pl.CostEstimate(
            flops=2 * tokens * width * kv, bytes_accessed=6 * tokens * width, transcendentals=0
        ),
        name="values_and_input_grad",
    )(owners, x, cot, inv, total, *arrays)


def send(block, where):
    return lax.ppermute(block, "fsdp", where)


def block_order(z, y):
    places = [(dz, dy) for dz in (0, 1) for dy in (0, -1, 1)] + [(0, 2), (1, 2)]
    return jnp.stack(
        [_index((z + dz) % NZ, k, (y + dy) % NY) for dz, dy in places for k in range(NX)]
    ).astype(jnp.int32)


def final_order(owners):
    near, others, far = owners[: 3 * NX], owners[3 * NX : 6 * NX], owners[6 * NX :]
    return jnp.concatenate([near, far[:NX], others, far[NX:]])


def body(
    layer_input,
    value_weight,
    norm_gain,
    cotangent,
    frag_global,
    frag_momentum,
    frag_snapshot,
    frag_local,
):
    x = layer_input[0]
    cot = cotangent[0]
    gain = norm_gain[0].astype(jnp.float32)[:, None]
    width = x.shape[1]
    rows, kv = value_weight[0].shape
    half = rows // 2
    factor = float(width) ** (-0.5)
    me = lax.axis_index("fsdp")
    place = jnp.reshape((me // NY) % NX, (1,)).astype(jnp.int32)
    f32 = jnp.float32

    def after(values, *others):
        return lax.optimization_barrier((values, others))[0]

    own = (value_weight[0].astype(f32) * gain).astype(jnp.bfloat16)
    slab = lax.all_to_all(
        jnp.broadcast_to(own, (NX, rows, kv)), "fsdp", 0, 0, axis_index_groups=X_GROUPS
    ).reshape(NX * rows, kv)
    inv, scaled = norm_and_scaled_cotangent(x, cot)

    chunk = NY * half
    sent = weight_grad_chunks(x, scaled, place, FIRST, jnp.bfloat16)
    got = [[send(sent[0], X_UP), send(sent[1], X_DOWN)]]
    below, above, other = send(slab, Y_UP), send(slab, Y_DOWN), send(slab, Z_SWAP)

    first = (got[0], below, above, other)
    messages = after(sent[2:], got[0])
    got.append([send(m, r) for m, r in zip(messages, (X_UP, X_DOWN))])
    message = after(other, below, above)
    other_below, other_above = send(message, Y_UP), send(message, Y_DOWN)

    owners = block_order(me // (NX * NY), me % NY)
    near, others = [slab, below, above], [other, other_below, other_above]
    kept = weight_grad_chunks(x, scaled, place, REST, f32)
    add = [[(chunk, [(0, way * chunk), (1 + way, 0)])] for way in (0, 1)]
    messages = after(assemble([kept[0], *got[0]], add), got[1])
    then = [[send(m, r) for m, r in zip(messages, (X_UP, X_DOWN))]]
    messages = after([below, other_above], other_below)
    far = [send(messages[0], Y_UP), send(messages[1], Y_DOWN)]
    messages = after(assemble([kept[2], *got[1]], add), then[0])
    then.append([send(m, r) for m, r in zip(messages, (X_UP, X_DOWN))])

    mine = after(frag_snapshot[0], *first)
    everyone = jnp.broadcast_to(mine, (lax.axis_size("rep"), *mine.shape))
    total = jnp.sum(lax.all_to_all(everyone, "rep", 0, 0).astype(f32), axis=0)
    mean_delta = frag_global - total * (1.0 / lax.axis_size("rep"))
    new_momentum = outer_beta * frag_momentum + mean_delta
    new_global = frag_global - outer_rate * (mean_delta + outer_beta * new_momentum)
    new_local = (
        merge_weight * frag_local[0].astype(f32) + (1.0 - merge_weight) * new_global
    ).astype(jnp.bfloat16)

    product = projection(x, [*near, *others], owners)

    arrays = [kept[1], *got[0], *then[0], kept[3], *got[1], *then[1]]
    segments = []
    for k in range(BLOCKS):
        z, start = k // NY, k % NY * half
        for n in (0, 5):
            came = [(n + 2 - z, chunk + start), (n + 3 + z, start)]
            segments.append((half, [(n, k * half), *came]))
    (ring,) = assemble(after(arrays, far, product), [segments])
    group = lax.all_to_all(ring.reshape(BLOCKS, rows, kv), "fsdp", 0, 0, axis_index_groups=ZY_GROUPS)

    values, input_grad = values_and_input_grad(
        x, [*near, far[0], *others, far[1]], final_order(owners), product, cot, inv
    )
    group = after(group, input_grad)
    weight_grad = jnp.sum(group.astype(f32), axis=0) * (factor * gain)
    return (
        values[None],
        input_grad[None],
        weight_grad[None],
        new_global,
        new_momentum,
        new_local[None],
    )


def solution(mesh):
    return jax.shard_map(
        body,
        mesh=mesh,
        in_specs=(
            P("rep", "fsdp", None),
            P("rep", "fsdp", None),
            P("rep", "fsdp"),
            P("rep", "fsdp", None),
            P("fsdp", None),
            P("fsdp", None),
            P("rep", "fsdp", None),
            P("rep", "fsdp", None),
        ),
        out_specs=(
            P("rep", "fsdp", None),
            P("rep", "fsdp", None),
            P("rep", "fsdp", None),
            P("fsdp", None),
            P("fsdp", None),
            P("rep", "fsdp", None),
        ),
        check_vma=False,
    )
```

```python
import functools

import jax
import jax.numpy as jnp
from jax import lax
from jax.experimental import pallas as pl
from jax.experimental.pallas import tpu as pltpu
from jax.sharding import PartitionSpec as P

epsilon = 1e-05
outer_rate = 0.7
outer_beta = 0.9
merge_weight = 0.5

NZ, NX, NY = 2, 4, 4
BLOCKS = NZ * NX
MIB = 1 << 20
VMEM_LIMIT = 56 * MIB


def _index(z, x, y):
    return (z * NX + x) * NY + y


ZY_GROUPS = [[_index(z, x, y) for z in range(NZ) for y in range(NY)] for x in range(NX)]
X_GROUPS = [[_index(z, x, y) for x in range(NX)] for z in range(NZ) for y in range(NY)]


def _shift(dz, dx, dy):
    return [
        (_index(z, x, y), _index((z + dz) % NZ, (x + dx) % NX, (y + dy) % NY))
        for z in range(NZ)
        for x in range(NX)
        for y in range(NY)
    ]


Z_SWAP = _shift(1, 0, 0)
X_UP, X_DOWN = _shift(0, 1, 0), _shift(0, -1, 0)
Y_UP, Y_DOWN = _shift(0, 0, 1), _shift(0, 0, -1)
MIB = 1 << 20
VMEM_LIMIT = 56 * MIB


def _index(z, x, y):
    return (z * NX + x) * NY + y


ZY_GROUPS = [[_index(z, x, y) for z in range(NZ) for y in range(NY)] for x in range(NX)]
ZX_GROUPS = [[_index(z, x, y) for z in range(NZ) for x in range(NX)] for y in range(NY)]


def _shift(dz, dx, dy):
    return [
        (_index(z, x, y), _index((z + dz) % NZ, (x + dx) % NX, (y + dy) % NY))
        for z in range(NZ)
        for x in range(NX)
        for y in range(NY)
    ]


Z_SWAP = _shift(1, 0, 0)
X_UP, X_DOWN = _shift(0, 1, 0), _shift(0, -1, 0)
Y_UP, Y_DOWN = _shift(0, 0, 1), _shift(0, 0, -1)
OTHER_CORE = [(0, 1), (1, 0), (2, 3), (3, 2)]
OTHER_Z = [(0, 2), (2, 0), (1, 3), (3, 1)]


HBM = pl.BlockSpec(memory_space=pl.ANY)
VMEM = pl.BlockSpec(memory_space=pltpu.VMEM)
SMEM = pl.BlockSpec(memory_space=pltpu.SMEM)
CHUNKS = 8

FIRST = ((2, 0), (1, 1), (2, 1), (NX - 1, 0))
REST = ((1, 0), (NX - 1, 1), (0, 0), (0, 1))


def first_kernel(width, todo, place_ref, x_ref, cot_ref, inv_ref, scaled_ref, *rest):
    outs, (held, stage, sems, store_sems) = rest[:4], rest[4:]
    chunks, rows = held.shape[:2]
    cols = width // BLOCKS
    part = cols // NY // 2

    def copy(k):
        return pltpu.make_async_copy(x_ref.at[pl.ds(k * rows, rows)], held.at[k], sems.at[k])

    def store(half, k):
        n = half * len(todo) + k
        where = outs[n // 2].at[pl.ds((n % 2) * NY * part, NY * part)]
        return pltpu.make_async_copy(stage.at[n], where, store_sems.at[n])

    for k in range(chunks):
        copy(k).start()
    for k in range(chunks):
        copy(k).wait()

        def add(c, total):
            wide = held[k, :, pl.ds(pl.multiple_of(c * 512, 512), 512)].astype(jnp.float32)
            squares = wide * wide
            return (
                total
                + (squares[:, :128] + squares[:, 128:256])
                + (squares[:, 256:384] + squares[:, 384:])
            )

        total = lax.fori_loop(0, width // 512, add, jnp.zeros((rows, 128), jnp.float32), unroll=4)
        inv = 1.0 / jnp.sqrt(jnp.sum(total, axis=1, keepdims=True) / width + epsilon)
        here = pl.ds(k * rows, rows)
        inv_ref[here, :] = jnp.broadcast_to(inv, (rows, 128))
        scaled_ref[here, :] = (cot_ref[here, :].astype(jnp.float32) * inv).astype(jnp.bfloat16)

    for k, (d, z) in enumerate(todo):
        j = z * NX + lax.rem(place_ref[0] + d, NX)
        for half in (0, 1):
            for p in range(NY):
                start = pl.multiple_of(j * cols + (2 * p + half) * part, part)
                piece = held[:, :, pl.ds(start, part)].reshape(chunks * rows, part)
                stage[half * len(todo) + k, p * part : (p + 1) * part, :] = lax.dot_general(
                    piece,
                    scaled_ref[...],
                    (((0,), (0,)), ((), ())),
                    preferred_element_type=jnp.float32,
                ).astype(stage.dtype)
            store(half, k).start()
    for k in range(len(todo)):
        for half in (0, 1):
            store(half, k).wait()


def norm_and_first_chunks(x, cot, place):
    tokens, width = x.shape
    kv = cot.shape[1]
    part = width // BLOCKS // NY // 2
    return pl.pallas_call(
        functools.partial(first_kernel, width, FIRST),
        in_specs=[SMEM, HBM, VMEM],
        out_specs=[VMEM, VMEM] + [HBM] * 4,
        out_shape=[
            jax.ShapeDtypeStruct((tokens, 128), jnp.float32),
            jax.ShapeDtypeStruct((tokens, kv), jnp.bfloat16),
        ]
        + [jax.ShapeDtypeStruct((2 * NY * part, kv), jnp.bfloat16)] * 4,
        scratch_shapes=[
            pltpu.VMEM((CHUNKS, tokens // CHUNKS, width), jnp.bfloat16),
            pltpu.VMEM((2 * len(FIRST), NY * part, kv), jnp.bfloat16),
            pltpu.SemaphoreType.DMA((CHUNKS,)),
            pltpu.SemaphoreType.DMA((2 * len(FIRST),)),
        ],
        compiler_params=pltpu.CompilerParams(vmem_limit_bytes=VMEM_LIMIT),
        cost_estimate=pl.CostEstimate(
            flops=tokens * width * kv, bytes_accessed=4 * tokens * width, transcendentals=0
        ),
        name="norm_and_first_chunks",
    )(place, x, cot)


def weight_grad_kernel(todo, place_ref, x_ref, scaled_ref, *rest):
    outs, (held, stage, load_sems, store_sems) = rest[:4], rest[4:]
    cols = held.shape[2]
    rows = cols // NY // 2
    x = place_ref[0]

    def load(k):
        d, z = todo[k]
        j = z * NX + lax.rem(x + d, NX)
        columns = pl.ds(pl.multiple_of(j * cols, cols), cols)
        return pltpu.make_async_copy(x_ref.at[:, columns], held.at[k], load_sems.at[k])

    def store(half, k):
        n = half * len(todo) + k
        where = outs[n // 2].at[pl.ds((n % 2) * NY * rows, NY * rows)]
        return pltpu.make_async_copy(stage.at[n], where, store_sems.at[n])

    for k in range(len(todo)):
        load(k).start()
    for k in range(len(todo)):
        load(k).wait()
        for half in (0, 1):
            for p in range(NY):
                stage[half * len(todo) + k, p * rows : (p + 1) * rows, :] = lax.dot_general(
                    held[k, :, (2 * p + half) * rows : (2 * p + half + 1) * rows],
                    scaled_ref[...],
                    (((0,), (0,)), ((), ())),
                    preferred_element_type=jnp.float32,
                ).astype(stage.dtype)
            store(half, k).start()
    for k in range(len(todo)):
        for half in (0, 1):
            store(half, k).wait()


def weight_grad_chunks(x, scaled, place, todo, dtype):
    tokens, width = x.shape
    kv = scaled.shape[1]
    cols = width // BLOCKS
    rows = cols // NY // 2
    return pl.pallas_call(
        functools.partial(weight_grad_kernel, todo),
        in_specs=[SMEM, HBM, VMEM],
        out_specs=[HBM] * 4,
        out_shape=[jax.ShapeDtypeStruct((2 * NY * rows, kv), dtype)] * 4,
        scratch_shapes=[
            pltpu.VMEM((len(todo), tokens, cols), jnp.bfloat16),
            pltpu.VMEM((2 * len(todo), NY * rows, kv), dtype),
            pltpu.SemaphoreType.DMA((len(todo),)),
            pltpu.SemaphoreType.DMA((2 * len(todo),)),
        ],
        compiler_params=pltpu.CompilerParams(vmem_limit_bytes=VMEM_LIMIT),
        cost_estimate=pl.CostEstimate(
            flops=tokens * width * kv, bytes_accessed=2 * tokens * width, transcendentals=0
        ),
        name="weight_grad_chunks",
    )(place, x, scaled)


def assemble_kernel(plan, rows_in, *refs):
    arrays, refs = refs[: len(rows_in)], refs[len(rows_in) :]
    outs, refs = refs[: len(plan)], refs[len(plan) :]
    stages, refs = refs[: len(plan)], refs[len(plan) :]
    *held, load_sems, store_sems = refs

    loads = []
    n = taken = 0
    for stage, segments in zip(stages, plan):
        start = 0
        for rows, sources in segments:
            here = []
            for array, first in sources:
                if len(sources) == 1:
                    target = stage.at[pl.ds(start, rows)]
                else:
                    target = held[taken]
                    taken += 1
                source = arrays[array].at[pl.ds(first, rows)]
                here.append((pltpu.make_async_copy(source, target, load_sems.at[n]), target))
                n += 1
            loads.append(here)
            start += rows
    for here in loads:
        for copy, _ in here:
            copy.start()
    stores = []
    k = 0
    for m, (out, stage, segments) in enumerate(zip(outs, stages, plan)):
        start = 0
        for rows, sources in segments:
            here = loads[k]
            k += 1
            for copy, _ in here:
                copy.wait()
            if len(sources) > 1:
                total = here[0][1][...].astype(jnp.float32)
                for _, target in here[1:]:
                    total = total + target[...].astype(jnp.float32)
                stage[start : start + rows, :] = total.astype(stage.dtype)
            start += rows
        stores.append(pltpu.make_async_copy(stage, out, store_sems.at[m]))
        stores[-1].start()
    for store in stores:
        store.wait()


def assemble(arrays, plan):
    kv = arrays[0].shape[1]
    sizes = [sum(rows for rows, _ in segments) for segments in plan]
    held = [
        pltpu.VMEM((rows, kv), arrays[array].dtype)
        for segments in plan
        for rows, sources in segments
        if len(sources) > 1
        for array, _ in sources
    ]
    copies = sum(len(sources) for segments in plan for _, sources in segments)
    return pl.pallas_call(
        functools.partial(assemble_kernel, plan, [a.shape[0] for a in arrays]),
        in_specs=[HBM] * len(arrays),
        out_specs=[HBM] * len(plan),
        out_shape=[jax.ShapeDtypeStruct((size, kv), jnp.bfloat16) for size in sizes],
        scratch_shapes=[pltpu.VMEM((size, kv), jnp.bfloat16) for size in sizes]
        + held
        + [pltpu.SemaphoreType.DMA((copies,)), pltpu.SemaphoreType.DMA((len(plan),))],
        compiler_params=pltpu.CompilerParams(vmem_limit_bytes=VMEM_LIMIT),
        cost_estimate=pl.CostEstimate(
            flops=sum(sizes) * kv, bytes_accessed=6 * sum(sizes) * kv, transcendentals=0
        ),
        name="assemble",
    )(*arrays)


def strip_copy(x_ref, strips, sems, owners_ref, k):
    rows = strips.shape[2]
    columns = pl.ds(pl.multiple_of(owners_ref[k] * rows, rows), rows)
    return pltpu.make_async_copy(x_ref.at[:, columns], strips.at[k], sems.at[k])


def projection_kernel(count, owners_ref, x_ref, *rest):
    *refs, total_ref, strips, held_w, w_sems, x_sems = rest
    rows = strips.shape[2]
    per_array = count // len(refs)

    def weight(k):
        block = refs[k // per_array].at[pl.ds((k % per_array) * rows, rows)]
        return pltpu.make_async_copy(block, held_w.at[k], w_sems.at[k])

    for k in range(count):
        strip_copy(x_ref, strips, x_sems, owners_ref, k).start()
        weight(k).start()
    for k in range(count):
        strip_copy(x_ref, strips, x_sems, owners_ref, k).wait()
        weight(k).wait()
        part = jnp.dot(strips[k], held_w[k], preferred_element_type=jnp.float32)
        total_ref[...] = part if k == 0 else total_ref[...] + part


def projection(x, arrays, owners):
    tokens, width = x.shape
    kv = arrays[0].shape[1]
    rows = width // BLOCKS // NY
    count = NX * len(arrays)
    return pl.pallas_call(
        functools.partial(projection_kernel, count),
        in_specs=[SMEM, HBM] + [HBM] * len(arrays),
        out_specs=VMEM,
        out_shape=jax.ShapeDtypeStruct((tokens, kv), jnp.float32),
        scratch_shapes=[
            pltpu.VMEM((count, tokens, rows), jnp.bfloat16),
            pltpu.VMEM((count, rows, kv), jnp.bfloat16),
            pltpu.SemaphoreType.DMA((count,)),
            pltpu.SemaphoreType.DMA((count,)),
        ],
        compiler_params=pltpu.CompilerParams(vmem_limit_bytes=VMEM_LIMIT),
        cost_estimate=pl.CostEstimate(
            flops=2 * tokens * rows * count * kv,
            bytes_accessed=4 * tokens * rows * count,
            transcendentals=0,
        ),
        name="projection",
    )(owners, x, *arrays)


def input_grad_kernel(width, factor, late, owners_ref, x_ref, cot_ref, inv_ref, total_ref, *rest):
    *refs, val_ref, out_ref, held_x, held_w, strips, stage, w_sems, x_sems, strip_sems, out_sems = rest
    tokens, cols = held_x.shape[1:]
    rows, kv = held_w.shape[1:]
    first = BLOCKS * NY - late
    per_side = len(refs) // NZ

    def weight(side, n, k):
        array = side * per_side + n
        y = lax.rem(owners_ref[array * NX], NY)
        where = held_w.at[(side * NX + k) * NY + y]
        return pltpu.make_async_copy(
            refs[array].at[pl.ds(k * rows, rows)], where, w_sems.at[array * NX + k]
        )

    def columns(ref, held, sems, side, k, out):
        j = owners_ref[side * per_side * NX + k] // NY
        where = ref.at[:, pl.ds(pl.multiple_of(j * cols, cols), cols)]
        step = side * NX + k
        if out:
            return pltpu.make_async_copy(held.at[step], where, sems.at[step])
        return pltpu.make_async_copy(where, held.at[step], sems.at[step])

    def strip(side, k):
        n = side * NX + k
        owner = owners_ref[(side * per_side + per_side - 1) * NX + k]
        where = x_ref.at[:, pl.ds(pl.multiple_of(owner * rows, rows), rows)]
        return pltpu.make_async_copy(where, strips.at[n], strip_sems.at[n])

    steps = [(side, k) for side in range(NZ) for k in range(NX)]
    for side, k in steps:
        strip(side, k).start()
        weight(side, per_side - 1, k).start()
    for side, k in steps:
        for n in range(per_side - 1):
            weight(side, n, k).start()
        columns(x_ref, held_x, x_sems, side, k, False).start()
    total = total_ref[...]
    for side, k in steps:
        strip(side, k).wait()
        weight(side, per_side - 1, k).wait()
        y = lax.rem(owners_ref[(side * per_side + per_side - 1) * NX], NY)
        total = total + jnp.dot(
            strips[side * NX + k],
            held_w[(side * NX + k) * NY + y],
            preferred_element_type=jnp.float32,
        )
    inv = inv_ref[:, :1]
    values = total * (factor * inv)
    val_ref[...] = values.astype(jnp.bfloat16)
    mean = jnp.sum(cot_ref[...].astype(jnp.float32) * values, axis=1, keepdims=True) / width
    shift = mean * inv * inv
    scale = factor * inv

    for side, k in steps:
        for n in range(per_side - 1):
            weight(side, n, k).wait()
        columns(x_ref, held_x, x_sems, side, k, False).wait()
        step = side * NX + k
        for n in range(NY):
            adjoint = lax.dot_general(
                cot_ref[...],
                held_w[step * NY + n],
                (((1,), (1,)), ((), ())),
                preferred_element_type=jnp.float32,
            )
            here = slice(n * rows, (n + 1) * rows)
            stage[step, :, here] = (
                adjoint * scale - held_x[step, :, here].astype(jnp.float32) * shift
            ).astype(jnp.bfloat16)
        columns(out_ref, stage, out_sems, side, k, True).start()
    for side, k in steps:
        columns(out_ref, stage, out_sems, side, k, True).wait()


def values_and_input_grad(x, arrays, owners, total, cot, inv):
    late = NZ * NX
    tokens, width = x.shape
    kv = cot.shape[1]
    cols = width // BLOCKS
    rows = cols // NY
    factor = float(width) ** (-0.5)
    return pl.pallas_call(
        functools.partial(input_grad_kernel, width, factor, late),
        in_specs=[SMEM, HBM, VMEM, VMEM, VMEM] + [HBM] * len(arrays),
        out_specs=[VMEM, HBM],
        out_shape=[
            jax.ShapeDtypeStruct((tokens, kv), jnp.bfloat16),
            jax.ShapeDtypeStruct((tokens, width), jnp.bfloat16),
        ],
        scratch_shapes=[
            pltpu.VMEM((BLOCKS, tokens, cols), jnp.bfloat16),
            pltpu.VMEM((BLOCKS * NY, rows, kv), jnp.bfloat16),
            pltpu.VMEM((late, tokens, rows), jnp.bfloat16),
            pltpu.VMEM((BLOCKS, tokens, cols), jnp.bfloat16),
            pltpu.SemaphoreType.DMA((BLOCKS * NY,)),
            pltpu.SemaphoreType.DMA((BLOCKS,)),
            pltpu.SemaphoreType.DMA((late,)),
            pltpu.SemaphoreType.DMA((BLOCKS,)),
        ],
        compiler_params=pltpu.CompilerParams(vmem_limit_bytes=VMEM_LIMIT),
        cost_estimate=pl.CostEstimate(
            flops=2 * tokens * width * kv, bytes_accessed=6 * tokens * width, transcendentals=0
        ),
        name="values_and_input_grad",
    )(owners, x, cot, inv, total, *arrays)


def send(block, where):
    return lax.ppermute(block, "fsdp", where)


def block_order(z, y):
    places = [(dz, dy) for dz in (0, 1) for dy in (0, -1, 1)] + [(0, 2), (1, 2)]
    return jnp.stack(
        [_index((z + dz) % NZ, k, (y + dy) % NY) for dz, dy in places for k in range(NX)]
    ).astype(jnp.int32)


def final_order(owners):
    near, others, far = owners[: 3 * NX], owners[3 * NX : 6 * NX], owners[6 * NX :]
    return jnp.concatenate([near, far[:NX], others, far[NX:]])


def body(
    layer_input,
    value_weight,
    norm_gain,
    cotangent,
    frag_global,
    frag_momentum,
    frag_snapshot,
    frag_local,
):
    x = layer_input[0]
    cot = cotangent[0]
    gain = norm_gain[0].astype(jnp.float32)[:, None]
    width = x.shape[1]
    rows, kv = value_weight[0].shape
    half = rows // 2
    factor = float(width) ** (-0.5)
    me = lax.axis_index("fsdp")
    place = jnp.reshape((me // NY) % NX, (1,)).astype(jnp.int32)
    f32 = jnp.float32

    def after(values, *others):
        return lax.optimization_barrier((values, others))[0]

    own = (value_weight[0].astype(f32) * gain).astype(jnp.bfloat16)
    slab = lax.all_to_all(
        jnp.broadcast_to(own, (NX, rows, kv)), "fsdp", 0, 0, axis_index_groups=X_GROUPS
    ).reshape(NX * rows, kv)
    inv, scaled, *sent = norm_and_first_chunks(x, cot, place)

    chunk = NY * half
    got = [[send(sent[0], X_UP), send(sent[1], X_DOWN)]]
    below, above, other = send(slab, Y_UP), send(slab, Y_DOWN), send(slab, Z_SWAP)

    first = (got[0], below, above, other)
    messages = after(sent[2:], got[0])
    got.append([send(m, r) for m, r in zip(messages, (X_UP, X_DOWN))])
    message = after(other, below, above)
    other_below, other_above = send(message, Y_UP), send(message, Y_DOWN)

    owners = block_order(me // (NX * NY), me % NY)
    near, others = [slab, below, above], [other, other_below, other_above]
    kept = weight_grad_chunks(x, scaled, place, REST, f32)
    add = [[(chunk, [(0, way * chunk), (1 + way, 0)])] for way in (0, 1)]
    messages = after(assemble([kept[0], *got[0]], add), got[1])
    then = [[send(m, r) for m, r in zip(messages, (X_UP, X_DOWN))]]
    messages = after([below, other_above], other_below)
    far = [send(messages[0], Y_UP), send(messages[1], Y_DOWN)]
    messages = after(assemble([kept[2], *got[1]], add), then[0])
    then.append([send(m, r) for m, r in zip(messages, (X_UP, X_DOWN))])

    mine = after(frag_snapshot[0], *first)
    everyone = jnp.broadcast_to(mine, (lax.axis_size("rep"), *mine.shape))
    total = jnp.sum(lax.all_to_all(everyone, "rep", 0, 0).astype(f32), axis=0)
    mean_delta = frag_global - total * (1.0 / lax.axis_size("rep"))
    new_momentum = outer_beta * frag_momentum + mean_delta
    new_global = frag_global - outer_rate * (mean_delta + outer_beta * new_momentum)
    new_local = (
        merge_weight * frag_local[0].astype(f32) + (1.0 - merge_weight) * new_global
    ).astype(jnp.bfloat16)

    product = projection(x, [*near, *others], owners)

    arrays = [kept[1], *got[0], *then[0], kept[3], *got[1], *then[1]]
    segments = []
    for k in range(BLOCKS):
        z, start = k // NY, k % NY * half
        for n in (0, 5):
            came = [(n + 2 - z, chunk + start), (n + 3 + z, start)]
            segments.append((half, [(n, k * half), *came]))
    (ring,) = assemble(after(arrays, far, product), [segments])
    group = lax.all_to_all(ring.reshape(BLOCKS, rows, kv), "fsdp", 0, 0, axis_index_groups=ZY_GROUPS)

    values, input_grad = values_and_input_grad(
        x, [*near, far[0], *others, far[1]], final_order(owners), product, cot, inv
    )
    group = after(group, input_grad)
    weight_grad = jnp.sum(group.astype(f32), axis=0) * (factor * gain)
    return (
        values[None],
        input_grad[None],
        weight_grad[None],
        new_global,
        new_momentum,
        new_local[None],
    )


def solution(mesh):
    return jax.shard_map(
        body,
        mesh=mesh,
        in_specs=(
            P("rep", "fsdp", None),
            P("rep", "fsdp", None),
            P("rep", "fsdp"),
            P("rep", "fsdp", None),
            P("fsdp", None),
            P("fsdp", None),
            P("rep", "fsdp", None),
            P("rep", "fsdp", None),
        ),
        out_specs=(
            P("rep", "fsdp", None),
            P("rep", "fsdp", None),
            P("rep", "fsdp", None),
            P("fsdp", None),
            P("fsdp", None),
            P("rep", "fsdp", None),
        ),
        check_vma=False,
    )
```
